32 devices in a mesh: group: 2 (over x), fsdp: 8 (over z, y), tp: 2 (over core).
Axes of the slice: x: 2, y: 2, z: 4, core: 2. Of those that a mesh axis runs over, the one named last changes fastest.
Arguments:
- inputs: bfloat16 [8192, 8192], P(('group', 'fsdp'), 'tp'), parts along dimension 0, may hold values from -6 to 6
- value_gradient: bfloat16 [8192, 1024], P(('group', 'fsdp'), 'tp'), parts along dimension 0, may hold values from -6 to 6
- fixed_projection_matrix: bfloat16 [8192, 1024], P('fsdp', 'tp'), may hold values from -0.0625 to 0.0625
- adapter_down_weight: bfloat16 [16, 16, 8192], P(('group', 'fsdp'), None, 'tp'), parts along dimension 0, may hold values from -0.0625 to 0.0625
- adapter_up_weight: bfloat16 [16, 16, 1024], P(('group', 'fsdp'), None, 'tp'), parts along dimension 0, may hold values from -0.1875 to 0.1875
- live_token_count: int32 [16], P('group'), parts along dimension 0, may hold values from 1 to 2048, as said below
- adapter_storage_row: int32 [16], P('group'), parts along dimension 0, may hold values from 0 to 7, each once
Outputs:
- input_gradient: bfloat16 [8192, 8192], P(('group', 'fsdp'), 'tp'), parts along dimension 0
- lowering_sensitivity: float32 [16, 16, 8192], P(('group', 'fsdp'), None, 'tp'), parts along dimension 0
- raising_sensitivity: float32 [16, 16, 1024], P(('group', 'fsdp'), None, 'tp'), parts along dimension 0
The draws below stay inside these ranges and needn't reach their ends.
There are 2 independent parts, one for each index of `group`. The reference program is written for one: setup_inputs(seed, part) draws one part's arguments, and reference() takes and returns one part's arrays. A program takes and returns all parts, laid end to end along the dimension named above; an argument that names none is the same for every part. Nothing has to cross between parts.
Inputs may be any that keep to these rules, and one draw needn't show every extreme that they name: `live_token_count`: the padded block counts ceil(c / 128) sum to 32; exactly one adapter has 16 blocks and 2048 live tokens, every adapter has at least one live token. `adapter_storage_row`: each storage row holds exactly one adapter.
All inputs are finite; a program needn't handle non-finite values.
Results may differ from the reference program's by a relative error of at most 0.0031.
Values may be sent and summed in bfloat16 or wider, within the bound.
A program may use at most 128 MiB of HBM per device.

```python
import jax
import jax.numpy as jnp
from jax import lax

MODEL_WIDTH = 8192
FACTOR_DIMENSION = 16
BLOCK = 128
ATTENTION_DEPTH = 1024
JOB_LOW_FACTORS = 8
TOKENS = 4096
BLOCKS = 32
MOST = 16


def draw_live_token_count(key, part):
    key = jax.random.fold_in(key, 11)
    key_rank, key_pad = jax.random.split(key, 2)
    ranking = jax.random.permutation(key_rank, JOB_LOW_FACTORS).astype(jnp.int32)
    spare = BLOCKS - JOB_LOW_FACTORS - (MOST - 1)
    share = spare // (JOB_LOW_FACTORS - 1)
    rest = spare % (JOB_LOW_FACTORS - 1)
    others = 1 + share + (ranking <= rest).astype(jnp.int32)
    blocks_of = jnp.where(ranking == 0, MOST, others).astype(jnp.int32)
    padding = jax.random.randint(key_pad, (JOB_LOW_FACTORS,), 0, BLOCK).astype(jnp.int32)
    padding = jnp.where(ranking == 0, 0, padding)
    return (blocks_of * BLOCK - padding).astype(jnp.int32)


def shard_levels(key, shape, cuts, least, high):
    factor_of = 1.0
    for position, parts in cuts:
        steps = jax.random.uniform(jax.random.fold_in(jax.random.fold_in(key, 6), position), (parts,), jnp.float32, least / len(cuts), high / len(cuts))
        factor_of = factor_of * jnp.repeat(jnp.exp(steps), shape[position] // parts).reshape((-1,) + (1,) * (len(shape) - 1 - position))
    return factor_of


def noise(rng, shape, spread, reach, shards=(), kind=jnp.bfloat16):
    drawn = spread * jax.random.normal(rng, shape, jnp.float32)
    if shards:
        drawn = drawn * shard_levels(rng, shape, shards, -0.22, 0.18)
    return jnp.clip(drawn, -reach, reach).astype(kind)


def setup_inputs(seed: int = 0, part: int = 0) -> dict:
    arg_keys = jax.random.split(jax.random.key(seed), 8)
    part_splits = jax.random.split(jax.random.fold_in(arg_keys[7], part), 8)
    inputs = noise(part_splits[0], (TOKENS, MODEL_WIDTH), 1.0, 6.0, ((0, 8), (1, 2)))
    value_gradient = noise(part_splits[1], (TOKENS, ATTENTION_DEPTH), 1.0, 6.0, ((0, 8), (1, 2)))
    fixed_projection_matrix = noise(arg_keys[2], (MODEL_WIDTH, ATTENTION_DEPTH), MODEL_WIDTH ** -0.5, 0.0625, ((0, 8), (1, 2)))
    adapter_down_weight = noise(part_splits[3], (JOB_LOW_FACTORS, FACTOR_DIMENSION, MODEL_WIDTH), MODEL_WIDTH ** -0.5, 0.0625, ((0, 8), (2, 2)))
    adapter_up_weight = noise(part_splits[4], (JOB_LOW_FACTORS, FACTOR_DIMENSION, ATTENTION_DEPTH), ATTENTION_DEPTH ** -0.5, 0.1875, ((0, 8), (2, 2)))
    live_token_count = draw_live_token_count(jax.random.fold_in(jax.random.fold_in(arg_keys[7], part), 71), part)
    adapter_storage_row = jax.random.permutation(part_splits[6], JOB_LOW_FACTORS).astype(jnp.int32)
    return dict(inputs=inputs, value_gradient=value_gradient, fixed_projection_matrix=fixed_projection_matrix, adapter_down_weight=adapter_down_weight, adapter_up_weight=adapter_up_weight, live_token_count=live_token_count, adapter_storage_row=adapter_storage_row)


adapter_scale = 2.0


def reference(inputs, value_gradient, fixed_projection_matrix, adapter_down_weight, adapter_up_weight, live_token_count, adapter_storage_row):
    counts = live_token_count.astype(jnp.int32)
    blocks_of = ((counts + BLOCK - 1) // BLOCK).astype(jnp.int32)
    stop_marks = jnp.cumsum(blocks_of).astype(jnp.int32)
    firsts = (stop_marks - blocks_of).astype(jnp.int32)
    segment_labels = jnp.arange(BLOCKS, dtype=jnp.int32)
    segment_pair_lookup = jnp.sum((stop_marks[None, :] <= segment_labels[:, None]).astype(jnp.int32), axis=1).astype(jnp.int32)
    offsets = jnp.arange(BLOCK, dtype=jnp.int32)

    def iteration(carry, segment):
        lowering_sensitivity, raising_sensitivity = carry
        factor_pair = segment_pair_lookup[segment]
        storage_row = adapter_storage_row[factor_pair].astype(jnp.int32)
        start = (segment * BLOCK).astype(jnp.int32)
        x_rows = lax.dynamic_slice_in_dim(inputs, start, BLOCK, 0)
        dy_rows = lax.dynamic_slice_in_dim(value_gradient, start, BLOCK, 0)
        live = (segment - firsts[factor_pair]) * BLOCK + offsets < counts[factor_pair]
        masked_tokens = jnp.where(live[:, None], dy_rows, jnp.zeros_like(dy_rows))
        down_weight_rows = lax.dynamic_index_in_dim(adapter_down_weight, storage_row, 0, keepdims=False)
        up_weight_rows = lax.dynamic_index_in_dim(adapter_up_weight, storage_row, 0, keepdims=False)
        reduced_activation = jnp.dot(x_rows, down_weight_rows.T, preferred_element_type=jnp.float32).astype(jnp.bfloat16)
        gradient_total = jnp.dot(masked_tokens, up_weight_rows.T, preferred_element_type=jnp.float32)
        narrow_backflow = (adapter_scale * gradient_total).astype(jnp.bfloat16)
        frozen_output = jnp.dot(masked_tokens, fixed_projection_matrix.T, preferred_element_type=jnp.float32)
        rows_out = (frozen_output + jnp.dot(narrow_backflow, down_weight_rows, preferred_element_type=jnp.float32)).astype(jnp.bfloat16)
        lowering_sensitivity = lowering_sensitivity.at[storage_row].add(jnp.dot(narrow_backflow.T, x_rows, preferred_element_type=jnp.float32))
        raising_sensitivity = raising_sensitivity.at[storage_row].add(adapter_scale * jnp.dot(reduced_activation.T, masked_tokens, preferred_element_type=jnp.float32))
        return (lowering_sensitivity, raising_sensitivity), rows_out

    lowering_beginning = jnp.zeros((JOB_LOW_FACTORS, FACTOR_DIMENSION, MODEL_WIDTH), jnp.float32)
    starting_raising_factor = jnp.zeros((JOB_LOW_FACTORS, FACTOR_DIMENSION, ATTENTION_DEPTH), jnp.float32)
    (lowering_sensitivity, raising_sensitivity), entry_lines = lax.scan(iteration, (lowering_beginning, starting_raising_factor), segment_labels)
    return entry_lines.reshape(TOKENS, MODEL_WIDTH), lowering_sensitivity, raising_sensitivity
```

```python
import functools

import jax
import jax.numpy as jnp
from jax import lax
from jax.experimental import pallas as pl
from jax.experimental.pallas import tpu as pltpu
from jax.sharding import PartitionSpec as P

BLOCK = 128


adapter_scale = 2.0


def shards(
    inputs,
    value_gradient,
    fixed_projection_matrix,
    adapter_down_weight,
    adapter_up_weight,
    live_token_count,
    adapter_storage_row,
):
    token_rows = inputs.shape[0]
    half_width = inputs.shape[1]
    heads_half = value_gradient.shape[1]
    adapter_total = live_token_count.shape[0]
    block_count = token_rows // BLOCK
    place_offset = lax.axis_index("fsdp")
    blocks_of = (live_token_count + BLOCK - 1) // BLOCK
    stop_marks = jnp.cumsum(blocks_of)
    firsts = stop_marks - blocks_of
    segment_labels = place_offset * block_count + jnp.arange(block_count, dtype=jnp.int32)
    owner_adapter = jnp.sum(
        (stop_marks[None, :] <= segment_labels[:, None]).astype(jnp.int32), axis=1
    )
    owner_hot = jnp.arange(adapter_total, dtype=jnp.int32)[None, :] == owner_adapter[:, None]
    count_block = jnp.sum(jnp.where(owner_hot, live_token_count[None, :], 0), axis=1)
    first_block = jnp.sum(jnp.where(owner_hot, firsts[None, :], 0), axis=1)
    position_segment = jnp.sum(jnp.where(owner_hot, adapter_storage_row[None, :], 0), axis=1)
    offsets = jnp.arange(BLOCK, dtype=jnp.int32)
    live = (segment_labels[:, None] - first_block[:, None]) * BLOCK + offsets[
        None, :
    ] < count_block[:, None]
    grad_blocks = value_gradient.reshape(block_count, BLOCK, heads_half)
    masked_tokens = jnp.where(live[:, :, None], grad_blocks, jnp.zeros_like(grad_blocks))
    source_segments = inputs.reshape(block_count, BLOCK, half_width)
    every_lowering_factor, up_all = (
        lax.all_gather(adapter_down_weight, "fsdp", axis=0, tiled=True),
        lax.all_gather(adapter_up_weight, "fsdp", axis=0, tiled=True),
    )
    picked_lowering_factor = jnp.take(every_lowering_factor, position_segment, axis=0)
    up_sel = jnp.take(up_all, position_segment, axis=0)
    low_part = jnp.einsum(
        "nsm,nxm->nsx", source_segments, picked_lowering_factor, preferred_element_type=jnp.float32
    )
    inner_grad_piece = jnp.einsum(
        "btk,brk->btr", masked_tokens, up_sel, preferred_element_type=jnp.float32
    )
    low_sum, middle_gradient_sum = lax.psum((low_part, inner_grad_piece), "tp")
    reduced_activation = low_sum.astype(jnp.bfloat16)
    narrow_backflow = (adapter_scale * middle_gradient_sum).astype(jnp.bfloat16)
    adapter_contribution = jnp.einsum(
        "njc,ncd->njd", narrow_backflow, picked_lowering_factor, preferred_element_type=jnp.float32
    )
    down_terms = jnp.einsum(
        "btr,bth->brh", narrow_backflow, source_segments, preferred_element_type=jnp.float32
    )
    up_contributions = adapter_scale * jnp.einsum(
        "btr,btk->brk", reduced_activation, masked_tokens, preferred_element_type=jnp.float32
    )
    slot_hot = (
        jnp.arange(adapter_total, dtype=jnp.int32)[None, :] == position_segment[:, None]
    ).astype(jnp.float32)
    dense_down = jnp.einsum("ba,brh->arh", slot_hot, down_terms, precision=lax.Precision.HIGHEST)
    dense_up = jnp.einsum(
        "ba,brk->ark", slot_hot, up_contributions, precision=lax.Precision.HIGHEST
    )
    sent_down = dense_down[:, None, :, :]
    sent_up = dense_up[:, None, :, :]
    recv_down, recv_up = (
        lax.all_to_all(sent_down, "fsdp", split_axis=0, concat_axis=1, tiled=True),
        lax.all_to_all(sent_up, "fsdp", split_axis=0, concat_axis=1, tiled=True),
    )
    lowering_sensitivity = jnp.sum(recv_down, axis=1)
    raising_sensitivity = jnp.sum(recv_up, axis=1)
    masked_rows = masked_tokens.reshape(token_rows, heads_half)
    every_feature = lax.dot_general(
        masked_rows,
        lax.all_gather(fixed_projection_matrix, "fsdp", axis=0, tiled=True),
        (((1,), (1,)), ((), ())),
        preferred_element_type=jnp.float32,
    )
    frozen_output = lax.psum_scatter(every_feature, "tp", scatter_dimension=1, tiled=True)
    input_gradient = (frozen_output + adapter_contribution.reshape(token_rows, half_width)).astype(
        jnp.bfloat16
    )
    return (input_gradient, lowering_sensitivity, raising_sensitivity)


F32 = jnp.float32
BF16 = jnp.bfloat16


def nt(a, b):
    return lax.dot_general(a, b, (((1,), (1,)), ((), ())), preferred_element_type=F32)


def fused_kernel(
    fsdp_total,
    x_ref, dv_ref, w_ref, a_ref, b_ref, cnt_ref, row_ref,
    ig_ref, lo_ref, ra_ref,
    wall, dvb, a_all, b_all, mask, gm, gm_t, psend, precv,
    lsend, lrecv, lfull, rsend, rrecv, osend, orecv,
    ch_s, ch_r, y_s, y_r, sb_s, sb_r, a_s, a_r, b_s, b_r,
    l_s, l_r, r_s, r_r, dv_s, dv_r, p_s, p_r, o_s, o_r,
):
    depth = fsdp_total // 2
    half = depth // 2
    tokens, width = x_ref.shape
    heads = dv_ref.shape[1]
    rank = a_ref.shape[1]
    slots = fsdp_total * rank
    rows = w_ref.shape[0] // 2
    g = lax.axis_index("group")
    f = lax.axis_index("fsdp")
    c = lax.axis_index("tp")
    z = f // 2
    y = f % 2
    lo = c * half
    sibling = (g, f, 1 - c)
    twin = (1 - g, f, c)

    def remote(src, dst, ss, rs, dev):
        return pltpu.make_async_remote_copy(
            src_ref=src, dst_ref=dst, send_sem=ss, recv_sem=rs,
            device_id=dev, device_id_type=pl.DeviceIdType.MESH,
        )

    barrier = pltpu.get_barrier_semaphore()
    for k in range(1, fsdp_total):
        pl.semaphore_signal(
            barrier, inc=1, device_id=(g, lax.rem(f + k, fsdp_total), c),
            device_id_type=pl.DeviceIdType.MESH,
        )
    for dev in (sibling, twin, (g, z * 2 + 1 - y, 1 - c)):
        pl.semaphore_signal(barrier, inc=1, device_id=dev, device_id_type=pl.DeviceIdType.MESH)

    wall[z, y, c] = w_ref[pl.ds(pl.multiple_of(g * rows, rows), rows), :]
    mine = pl.ds(pl.multiple_of(f * rank, rank), rank)
    a_all[mine, :] = a_ref[0]
    b_all[mine, :] = b_ref[0]
    token = f * tokens + lax.broadcasted_iota(jnp.int32, (tokens, slots), 0)
    lane_row = lax.broadcasted_iota(jnp.int32, (tokens, slots), 1) // rank
    start = jnp.int32(0)
    alive = jnp.zeros((tokens, slots), F32)
    any_live = jnp.zeros((tokens, slots), F32)
    for a in range(fsdp_total):
        count = cnt_ref[a]
        blocks = (count + (BLOCK - 1)) // BLOCK
        inside = jnp.where((token >= start) & (token < start + count), 1.0, 0.0)
        any_live = any_live + inside
        alive = alive + jnp.where(lane_row == row_ref[a], inside, 0.0)
        start = start + blocks * BLOCK
    mask[...] = alive
    live_column = any_live[:, :1]
    dvb[0, c] = jnp.where(live_column > 0.5, dv_ref[...].astype(F32), 0.0).astype(BF16)

    pl.semaphore_wait(barrier, fsdp_total + 2)

    def dv_copy(i):
        if i == 0:
            return remote(dvb.at[0, c], dvb.at[0, c], dv_s.at[0], dv_r.at[0], sibling)
        if i == 1:
            return remote(dvb.at[0, c], dvb.at[1, c], dv_s.at[1], dv_r.at[1], twin)
        return remote(dvb.at[1, c], dvb.at[1, c], dv_s.at[2], dv_r.at[2], sibling)

    def piece(zp):
        return wall.at[zp, y, c]

    def chain_copy(zp, up):
        to = z + 1 if up else z - 1
        return remote(piece(zp), piece(zp), ch_s.at[zp, 1 if up else 0], ch_r.at[zp], (g, to * 2 + y, c))

    def y_copy(zp):
        core = zp // half
        return remote(piece(zp), piece(zp), y_s.at[zp], y_r.at[zp, c], (g, z * 2 + 1 - y, core))

    def sib_copy(zp):
        return remote(piece(zp), piece(zp), sb_s.at[zp], sb_r.at[zp], sibling)

    def b_copy(j):
        return remote(b_all.at[mine, :], b_all.at[mine, :], b_s.at[j], b_r.at[f], (g, j, c))

    def a_copy(j):
        return remote(a_all.at[mine, :], a_all.at[mine, :], a_s.at[j], a_r.at[f], (g, j, c))

    def peers(fn):
        def step(k, carry):
            fn(lax.rem(f + k, fsdp_total))
            return carry
        lax.fori_loop(1, fsdp_total, step, 0)

    def rank_rows(j):
        return pl.ds(pl.multiple_of(j * rank, rank), rank)

    def wait_in(dst, sem):
        remote(dst, dst, sem, sem, sibling).wait_recv()

    def spread(zp):
        y_copy(zp).start()

        @pl.when(zp // half != c)
        def _():
            sib_copy(zp).start()

    dv_copy(0).start()
    peers(lambda j: b_copy(j).start())

    @pl.when(z < depth - 1)
    def _():
        chain_copy(z, True).start()

    @pl.when(z > 0)
    def _():
        chain_copy(z, False).start()

    dv_copy(1).start()
    spread(z)
    peers(lambda j: a_copy(j).start())

    peers(lambda j: wait_in(b_all.at[rank_rows(j), :], b_r.at[j]))
    psend[0] = nt(dvb[0, c], b_all[...])
    gm_copy = remote(psend.at[0], precv.at[0], p_s.at[0], p_r.at[0], sibling)
    gm_copy.start()
    gm_copy.wait_recv()
    total = adapter_scale * (psend[0] + precv[0])
    total = jnp.where(mask[...] > 0.5, total, 0.0)
    gm[...] = total.astype(BF16)
    gm_t[...] = total.T.astype(BF16)

    chunk = 512

    def lower(i, carry):
        cols = pl.ds(pl.multiple_of(i * chunk, chunk), chunk)
        term = jnp.dot(gm_t[...], x_ref[:, cols], preferred_element_type=F32)
        lfull[:, cols] = term
        lsend[:, cols] = term.astype(BF16)
        return carry

    lax.fori_loop(0, width // chunk, lower, 0)

    def l_copy(j):
        return remote(lsend.at[rank_rows(j), :], lrecv.at[mine, :], l_s.at[j], l_r.at[f], (g, j, c))

    peers(lambda j: l_copy(j).start())

    wait_in(dvb.at[1, c], dv_r.at[1])
    dv_copy(2).start()

    peers(lambda j: wait_in(a_all.at[rank_rows(j), :], a_r.at[j]))
    psend[1] = jnp.zeros((tokens, slots), F32)

    def low_step(i, carry):
        cols = pl.ds(pl.multiple_of(i * chunk, chunk), chunk)
        psend[1] = psend[1] + nt(x_ref[:, cols], a_all[:, cols])
        return carry

    lax.fori_loop(0, width // chunk, low_step, 0)
    low_copy = remote(psend.at[1], precv.at[1], p_s.at[1], p_r.at[1], sibling)
    low_copy.start()
    low_copy.wait_recv()
    low = jnp.where(mask[...] > 0.5, psend[1] + precv[1], 0.0)
    up_term = adapter_scale * jnp.dot(low.T.astype(BF16), dvb[0, c], preferred_element_type=F32)
    rsend[...] = up_term

    def r_copy(j):
        return remote(rsend.at[rank_rows(j), :], rrecv.at[mine, :], r_s.at[j], r_r.at[f], (g, j, c))

    peers(lambda j: r_copy(j).start())
    wait_in(dvb.at[0, 1 - c], dv_r.at[0])
    wait_in(dvb.at[1, 1 - c], dv_r.at[2])

    def o_copy(tile):
        return remote(osend.at[tile], orecv.at[tile], o_s.at[tile], o_r.at[tile], twin)

    def columns(tile, which):
        return pl.ds(pl.multiple_of(tile * (2 * rows) + which * rows, rows), rows)

    def tiles(zt):
        wait_in(wall.at[zt, y, 1 - c], sb_r.at[zt])
        for other in (0, 1):
            yp = 1 - y if other else y
            if other:
                wait_in(wall.at[zt, yp, 0], y_r.at[zt, 0])
                wait_in(wall.at[zt, yp, 1], y_r.at[zt, 1])
            tile = (zt - lo) * 2 + yp
            osend[tile] = (nt(dvb[1, 0], wall[zt, yp, 0]) + nt(dvb[1, 1], wall[zt, yp, 1])).astype(BF16)
            o_copy(tile).start()
            cols = columns(tile, g)
            ig_ref[:, cols] = (
                nt(dvb[0, 0], wall[zt, yp, 0])
                + nt(dvb[0, 1], wall[zt, yp, 1])
                + jnp.dot(gm[...], a_all[:, cols], preferred_element_type=F32)
            ).astype(BF16)

    def in_half(zp):
        return (zp >= lo) & (zp < lo + half)

    def step(d, carry):
        @pl.when(z - d >= 0)
        def _():
            wait_in(piece(z - d), ch_r.at[z - d])

            @pl.when(z < depth - 1)
            def _():
                chain_copy(z - d, True).start()

            spread(z - d)

        @pl.when(z + d < depth)
        def _():
            wait_in(piece(z + d), ch_r.at[z + d])

            @pl.when(z > 0)
            def _():
                chain_copy(z + d, False).start()

            spread(z + d)

        zt = jnp.where(in_half(z + d - 1), z + d - 1, z - d + 1)

        @pl.when(in_half(zt))
        def _():
            tiles(zt)

        return carry

    lax.fori_loop(1, depth + 1, step, 0)

    def finish(tile, carry):
        wait_in(orecv.at[tile], o_r.at[tile])
        cols = columns(tile, 1 - g)
        ig_ref[:, cols] = (
            orecv[tile].astype(F32)
            + jnp.dot(gm[...], a_all[:, cols], preferred_element_type=F32)
        ).astype(BF16)
        return carry

    lax.fori_loop(0, 2 * half, finish, 0)

    lo_ref[0] = lfull[mine, :]
    ra_ref[0] = rsend[mine, :]

    def add_terms(j):
        wait_in(lrecv.at[rank_rows(j), :], l_r.at[j])
        lo_ref[0] = lo_ref[0] + lrecv[rank_rows(j), :].astype(F32)
        wait_in(rrecv.at[rank_rows(j), :], r_r.at[j])
        ra_ref[0] = ra_ref[0] + rrecv[rank_rows(j), :]

    peers(add_terms)

    for i in range(3):
        dv_copy(i).wait_send()
    gm_copy.wait_send()
    low_copy.wait_send()

    def sent(j):
        a_copy(j).wait_send()
        b_copy(j).wait_send()
        l_copy(j).wait_send()
        r_copy(j).wait_send()

    peers(sent)

    def sent_tile(tile, carry):
        o_copy(tile).wait_send()
        return carry

    lax.fori_loop(0, 2 * half, sent_tile, 0)

    def sent_piece(zp, carry):
        @pl.when((zp <= z) & (z < depth - 1))
        def _():
            chain_copy(zp, True).wait_send()

        @pl.when((zp >= z) & (z > 0))
        def _():
            chain_copy(zp, False).wait_send()

        y_copy(zp).wait_send()

        @pl.when(zp // half != c)
        def _():
            sib_copy(zp).wait_send()

        return carry

    lax.fori_loop(0, depth, sent_piece, 0)


def fused(fsdp_total, x, dv, w, a, b, counts, storage):
    tokens, width = x.shape
    heads = dv.shape[1]
    rank = a.shape[1]
    slots = fsdp_total * rank
    depth = fsdp_total // 2
    half = depth // 2
    rows = w.shape[0] // 2
    vmem = pl.BlockSpec(memory_space=pltpu.VMEM)
    smem = pl.BlockSpec(memory_space=pltpu.SMEM)
    dma = pltpu.SemaphoreType.DMA
    n = fsdp_total
    return pl.pallas_call(
        functools.partial(fused_kernel, fsdp_total),
        out_shape=(
            jax.ShapeDtypeStruct((tokens, width), BF16),
            jax.ShapeDtypeStruct((1, rank, width), F32),
            jax.ShapeDtypeStruct((1, rank, heads), F32),
        ),
        in_specs=[vmem] * 5 + [smem] * 2,
        out_specs=(vmem,) * 3,
        scratch_shapes=[
            pltpu.VMEM((depth, 2, 2, rows, heads), BF16),
            pltpu.VMEM((2, 2, tokens, heads), BF16),
            pltpu.VMEM((slots, width), BF16),
            pltpu.VMEM((slots, heads), BF16),
            pltpu.VMEM((tokens, slots), F32),
            pltpu.VMEM((tokens, slots), BF16),
            pltpu.VMEM((slots, tokens), BF16),
            pltpu.VMEM((2, tokens, slots), F32),
            pltpu.VMEM((2, tokens, slots), F32),
            pltpu.VMEM((slots, width), BF16),
            pltpu.VMEM((slots, width), BF16),
            pltpu.VMEM((slots, width), F32),
            pltpu.VMEM((slots, heads), F32),
            pltpu.VMEM((slots, heads), F32),
            pltpu.VMEM((2 * half, tokens, rows), BF16),
            pltpu.VMEM((2 * half, tokens, rows), BF16),
            dma((depth, 2)), dma((depth,)),
            dma((depth,)), dma((depth, 2)),
            dma((depth,)), dma((depth,)),
            dma((n,)), dma((n,)), dma((n,)), dma((n,)),
            dma((n,)), dma((n,)), dma((n,)), dma((n,)),
            dma((3,)), dma((3,)), dma((2,)), dma((2,)),
            dma((2 * half,)), dma((2 * half,)),
        ],
        compiler_params=pltpu.CompilerParams(
            collective_id=0, has_side_effects=True, vmem_limit_bytes=60 * 1024 * 1024
        ),
    )(x, dv, w, a, b, counts, storage)


def solution(mesh):
    in_specs = (
        P(("group", "fsdp"), "tp"),
        P(("group", "fsdp"), "tp"),
        P("fsdp", "tp"),
        P(("group", "fsdp"), None, "tp"),
        P(("group", "fsdp"), None, "tp"),
        P("group"),
        P("group"),
    )
    out_specs = (
        P(("group", "fsdp"), "tp"),
        P(("group", "fsdp"), None, "tp"),
        P(("group", "fsdp"), None, "tp"),
    )
    shape = dict(mesh.shape)
    paired = shape["group"] == 2 and shape["fsdp"] == 8 and shape["tp"] == 2
    body = functools.partial(fused, shape["fsdp"]) if paired else shards
    return jax.shard_map(body, mesh=mesh, in_specs=in_specs, out_specs=out_specs, check_vma=False)
```

```python
import functools

import jax
import jax.numpy as jnp
from jax import lax
from jax.experimental import pallas as pl
from jax.experimental.pallas import tpu as pltpu
from jax.sharding import PartitionSpec as P

BLOCK = 128


adapter_scale = 2.0


def shards(
    inputs,
    value_gradient,
    fixed_projection_matrix,
    adapter_down_weight,
    adapter_up_weight,
    live_token_count,
    adapter_storage_row,
):
    token_rows = inputs.shape[0]
    half_width = inputs.shape[1]
    heads_half = value_gradient.shape[1]
    adapter_total = live_token_count.shape[0]
    block_count = token_rows // BLOCK
    place_offset = lax.axis_index("fsdp")
    blocks_of = (live_token_count + BLOCK - 1) // BLOCK
    stop_marks = jnp.cumsum(blocks_of)
    firsts = stop_marks - blocks_of
    segment_labels = place_offset * block_count + jnp.arange(block_count, dtype=jnp.int32)
    owner_adapter = jnp.sum(
        (stop_marks[None, :] <= segment_labels[:, None]).astype(jnp.int32), axis=1
    )
    owner_hot = jnp.arange(adapter_total, dtype=jnp.int32)[None, :] == owner_adapter[:, None]
    count_block = jnp.sum(jnp.where(owner_hot, live_token_count[None, :], 0), axis=1)
    first_block = jnp.sum(jnp.where(owner_hot, firsts[None, :], 0), axis=1)
    position_segment = jnp.sum(jnp.where(owner_hot, adapter_storage_row[None, :], 0), axis=1)
    offsets = jnp.arange(BLOCK, dtype=jnp.int32)
    live = (segment_labels[:, None] - first_block[:, None]) * BLOCK + offsets[
        None, :
    ] < count_block[:, None]
    grad_blocks = value_gradient.reshape(block_count, BLOCK, heads_half)
    masked_tokens = jnp.where(live[:, :, None], grad_blocks, jnp.zeros_like(grad_blocks))
    source_segments = inputs.reshape(block_count, BLOCK, half_width)
    every_lowering_factor, up_all = (
        lax.all_gather(adapter_down_weight, "fsdp", axis=0, tiled=True),
        lax.all_gather(adapter_up_weight, "fsdp", axis=0, tiled=True),
    )
    picked_lowering_factor = jnp.take(every_lowering_factor, position_segment, axis=0)
    up_sel = jnp.take(up_all, position_segment, axis=0)
    low_part = jnp.einsum(
        "nsm,nxm->nsx", source_segments, picked_lowering_factor, preferred_element_type=jnp.float32
    )
    inner_grad_piece = jnp.einsum(
        "btk,brk->btr", masked_tokens, up_sel, preferred_element_type=jnp.float32
    )
    low_sum, middle_gradient_sum = lax.psum((low_part, inner_grad_piece), "tp")
    reduced_activation = low_sum.astype(jnp.bfloat16)
    narrow_backflow = (adapter_scale * middle_gradient_sum).astype(jnp.bfloat16)
    adapter_contribution = jnp.einsum(
        "njc,ncd->njd", narrow_backflow, picked_lowering_factor, preferred_element_type=jnp.float32
    )
    down_terms = jnp.einsum(
        "btr,bth->brh", narrow_backflow, source_segments, preferred_element_type=jnp.float32
    )
    up_contributions = adapter_scale * jnp.einsum(
        "btr,btk->brk", reduced_activation, masked_tokens, preferred_element_type=jnp.float32
    )
    slot_hot = (
        jnp.arange(adapter_total, dtype=jnp.int32)[None, :] == position_segment[:, None]
    ).astype(jnp.float32)
    dense_down = jnp.einsum("ba,brh->arh", slot_hot, down_terms, precision=lax.Precision.HIGHEST)
    dense_up = jnp.einsum(
        "ba,brk->ark", slot_hot, up_contributions, precision=lax.Precision.HIGHEST
    )
    sent_down = dense_down[:, None, :, :]
    sent_up = dense_up[:, None, :, :]
    recv_down, recv_up = (
        lax.all_to_all(sent_down, "fsdp", split_axis=0, concat_axis=1, tiled=True),
        lax.all_to_all(sent_up, "fsdp", split_axis=0, concat_axis=1, tiled=True),
    )
    lowering_sensitivity = jnp.sum(recv_down, axis=1)
    raising_sensitivity = jnp.sum(recv_up, axis=1)
    masked_rows = masked_tokens.reshape(token_rows, heads_half)
    every_feature = lax.dot_general(
        masked_rows,
        lax.all_gather(fixed_projection_matrix, "fsdp", axis=0, tiled=True),
        (((1,), (1,)), ((), ())),
        preferred_element_type=jnp.float32,
    )
    frozen_output = lax.psum_scatter(every_feature, "tp", scatter_dimension=1, tiled=True)
    input_gradient = (frozen_output + adapter_contribution.reshape(token_rows, half_width)).astype(
        jnp.bfloat16
    )
    return (input_gradient, lowering_sensitivity, raising_sensitivity)


F32 = jnp.float32
BF16 = jnp.bfloat16


def nt(a, b):
    return lax.dot_general(a, b, (((1,), (1,)), ((), ())), preferred_element_type=F32)


def fused_kernel(
    fsdp_total,
    x_ref, dv_ref, w_ref, a_ref, b_ref, cnt_ref, row_ref,
    ig_ref, lo_ref, ra_ref,
    wall, dvb, a_all, b_all, mask, gm, gm_t, psend, precv,
    lsend, lcross, lrecv, lfull, rsend, rrecv, osend, orecv,
    ch_s, ch_r, y_s, y_r, sb_s, sb_r, a_s, a_r, b_s, b_r,
    l_s, lc_r, l_r, r_s, r_r, dv_s, dv_r, p_s, p_r, o_s, o_r,
):
    depth = fsdp_total // 2
    half = depth // 2
    tokens, width = x_ref.shape
    heads = dv_ref.shape[1]
    rank = a_ref.shape[1]
    slots = fsdp_total * rank
    rows = w_ref.shape[0] // 2
    g = lax.axis_index("group")
    f = lax.axis_index("fsdp")
    c = lax.axis_index("tp")
    z = f // 2
    y = f % 2
    lo = c * half
    sibling = (g, f, 1 - c)
    twin = (1 - g, f, c)

    def remote(src, dst, ss, rs, dev):
        return pltpu.make_async_remote_copy(
            src_ref=src, dst_ref=dst, send_sem=ss, recv_sem=rs,
            device_id=dev, device_id_type=pl.DeviceIdType.MESH,
        )

    barrier = pltpu.get_barrier_semaphore()
    for k in range(1, fsdp_total):
        pl.semaphore_signal(
            barrier, inc=1, device_id=(g, lax.rem(f + k, fsdp_total), c),
            device_id_type=pl.DeviceIdType.MESH,
        )
    for dev in (sibling, twin, (g, z * 2 + 1 - y, 1 - c)):
        pl.semaphore_signal(barrier, inc=1, device_id=dev, device_id_type=pl.DeviceIdType.MESH)

    wall[z, y, c] = w_ref[pl.ds(pl.multiple_of(g * rows, rows), rows), :]
    mine = pl.ds(pl.multiple_of(f * rank, rank), rank)
    a_all[mine, :] = a_ref[0]
    b_all[mine, :] = b_ref[0]
    token = f * tokens + lax.broadcasted_iota(jnp.int32, (tokens, slots), 0)
    lane_row = lax.broadcasted_iota(jnp.int32, (tokens, slots), 1) // rank
    start = jnp.int32(0)
    alive = jnp.zeros((tokens, slots), F32)
    any_live = jnp.zeros((tokens, slots), F32)
    for a in range(fsdp_total):
        count = cnt_ref[a]
        blocks = (count + (BLOCK - 1)) // BLOCK
        inside = jnp.where((token >= start) & (token < start + count), 1.0, 0.0)
        any_live = any_live + inside
        alive = alive + jnp.where(lane_row == row_ref[a], inside, 0.0)
        start = start + blocks * BLOCK
    mask[...] = alive
    live_column = any_live[:, :1]
    dvb[0, c] = jnp.where(live_column > 0.5, dv_ref[...].astype(F32), 0.0).astype(BF16)

    pl.semaphore_wait(barrier, fsdp_total + 2)

    def dv_copy(i):
        if i == 0:
            return remote(dvb.at[0, c], dvb.at[0, c], dv_s.at[0], dv_r.at[0], sibling)
        if i == 1:
            return remote(dvb.at[0, c], dvb.at[1, c], dv_s.at[1], dv_r.at[1], twin)
        return remote(dvb.at[1, c], dvb.at[1, c], dv_s.at[2], dv_r.at[2], sibling)

    def piece(zp):
        return wall.at[zp, y, c]

    def chain_copy(zp, up):
        to = z + 1 if up else z - 1
        return remote(piece(zp), piece(zp), ch_s.at[zp, 1 if up else 0], ch_r.at[zp], (g, to * 2 + y, c))

    def y_copy(zp):
        core = zp // half
        return remote(piece(zp), piece(zp), y_s.at[zp], y_r.at[zp, c], (g, z * 2 + 1 - y, core))

    def sib_copy(zp):
        return remote(piece(zp), piece(zp), sb_s.at[zp], sb_r.at[zp], sibling)

    def b_copy(j):
        return remote(b_all.at[mine, :], b_all.at[mine, :], b_s.at[j], b_r.at[f], (g, j, c))

    opposite = z * 2 + 1 - y

    def a_copy(s, j):
        part = a_all.at[rank_rows(s), :]
        return remote(part, part, a_s.at[j * 2 + s % 2], a_r.at[s], (g, j, c))

    def levels(fn):
        def step(k, carry):
            fn(lax.rem(z + k, depth))
            return carry
        lax.fori_loop(1, depth, step, 0)

    def peers(fn):
        def step(k, carry):
            fn(lax.rem(f + k, fsdp_total))
            return carry
        lax.fori_loop(1, fsdp_total, step, 0)

    def rank_rows(j):
        return pl.ds(pl.multiple_of(j * rank, rank), rank)

    def wait_in(dst, sem):
        remote(dst, dst, sem, sem, sibling).wait_recv()

    def spread(zp):
        y_copy(zp).start()

        @pl.when(zp // half != c)
        def _():
            sib_copy(zp).start()

    dv_copy(0).start()
    peers(lambda j: b_copy(j).start())

    @pl.when(z < depth - 1)
    def _():
        chain_copy(z, True).start()

    @pl.when(z > 0)
    def _():
        chain_copy(z, False).start()

    dv_copy(1).start()
    spread(z)
    a_copy(f, opposite).start()
    levels(lambda zp: a_copy(f, zp * 2 + y).start())

    peers(lambda j: wait_in(b_all.at[rank_rows(j), :], b_r.at[j]))
    psend[0] = nt(dvb[0, c], b_all[...])
    gm_copy = remote(psend.at[0], precv.at[0], p_s.at[0], p_r.at[0], sibling)
    gm_copy.start()
    gm_copy.wait_recv()
    total = adapter_scale * (psend[0] + precv[0])
    total = jnp.where(mask[...] > 0.5, total, 0.0)
    gm[...] = total.astype(BF16)
    gm_t[...] = total.T.astype(BF16)

    chunk = 512

    def lower(i, carry):
        cols = pl.ds(pl.multiple_of(i * chunk, chunk), chunk)
        term = jnp.dot(gm_t[...], x_ref[:, cols], preferred_element_type=F32)
        lfull[:, cols] = term
        lsend[:, cols] = term.astype(BF16)
        return carry

    lax.fori_loop(0, width // chunk, lower, 0)

    def l_cross(zp):
        return remote(
            lsend.at[rank_rows(zp * 2 + 1 - y), :], lcross.at[zp], l_s.at[zp * 2 + 1 - y], lc_r.at[zp], (g, opposite, c)
        )

    def l_copy(zp):
        return remote(
            lsend.at[rank_rows(zp * 2 + y), :], lrecv.at[z], l_s.at[zp * 2 + y], l_r.at[z], (g, zp * 2 + y, c)
        )

    levels(lambda zp: l_cross(zp).start())
    l_cross(z).start()

    wait_in(a_all.at[rank_rows(opposite), :], a_r.at[opposite])
    levels(lambda zp: a_copy(opposite, zp * 2 + y).start())

    wait_in(dvb.at[1, c], dv_r.at[1])
    dv_copy(2).start()

    wait_in(dvb.at[0, 1 - c], dv_r.at[0])
    wait_in(dvb.at[1, 1 - c], dv_r.at[2])

    def join(zp):
        wait_in(lcross.at[zp], lc_r.at[zp])
        place = rank_rows(zp * 2 + y)
        lfull[place, :] = lfull[place, :] + lcross[zp].astype(F32)
        lsend[place, :] = lfull[place, :].astype(BF16)
        l_copy(zp).start()

    def join_all():
        levels(join)
        wait_in(lcross.at[z], lc_r.at[z])
        lfull[mine, :] = lfull[mine, :] + lcross[z].astype(F32)

    def o_copy(tile):
        return remote(osend.at[tile], orecv.at[tile], o_s.at[tile], o_r.at[tile], twin)

    def columns(tile, which):
        return pl.ds(pl.multiple_of(tile * (2 * rows) + which * rows, rows), rows)

    def tiles(zt):
        wait_in(wall.at[zt, y, 1 - c], sb_r.at[zt])
        for other in (0, 1):
            yp = 1 - y if other else y
            if other:
                wait_in(wall.at[zt, yp, 0], y_r.at[zt, 0])
                wait_in(wall.at[zt, yp, 1], y_r.at[zt, 1])
            tile = (zt - lo) * 2 + yp
            osend[tile] = (nt(dvb[1, 0], wall[zt, yp, 0]) + nt(dvb[1, 1], wall[zt, yp, 1])).astype(BF16)
            o_copy(tile).start()

    def in_half(zp):
        return (zp >= lo) & (zp < lo + half)

    def step(d, carry):
        @pl.when(z - d >= 0)
        def _():
            wait_in(piece(z - d), ch_r.at[z - d])

            @pl.when(z < depth - 1)
            def _():
                chain_copy(z - d, True).start()

            spread(z - d)

        @pl.when(z + d < depth)
        def _():
            wait_in(piece(z + d), ch_r.at[z + d])

            @pl.when(z > 0)
            def _():
                chain_copy(z + d, False).start()

            spread(z + d)

        zt = jnp.where(in_half(z + d - 1), z + d - 1, z - d + 1)

        @pl.when(in_half(zt))
        def _():
            tiles(zt)

        return carry

    lax.fori_loop(1, 2, step, 0)
    join_all()
    lax.fori_loop(2, depth, step, 0)

    levels(lambda zp: wait_in(a_all.at[rank_rows(zp * 2 + y), :], a_r.at[zp * 2 + y]))
    levels(lambda zp: wait_in(a_all.at[rank_rows(zp * 2 + 1 - y), :], a_r.at[zp * 2 + 1 - y]))
    psend[1] = jnp.zeros((tokens, slots), F32)

    def low_step(i, carry):
        cols = pl.ds(pl.multiple_of(i * chunk, chunk), chunk)
        psend[1] = psend[1] + nt(x_ref[:, cols], a_all[:, cols])
        return carry

    lax.fori_loop(0, width // chunk, low_step, 0)
    low_copy = remote(psend.at[1], precv.at[1], p_s.at[1], p_r.at[1], sibling)
    low_copy.start()
    low_copy.wait_recv()
    low = jnp.where(mask[...] > 0.5, psend[1] + precv[1], 0.0)
    up_term = adapter_scale * jnp.dot(low.T.astype(BF16), dvb[0, c], preferred_element_type=F32)
    rsend[...] = up_term

    def r_copy(j):
        return remote(rsend.at[rank_rows(j), :], rrecv.at[mine, :], r_s.at[j], r_r.at[f], (g, j, c))

    peers(lambda j: r_copy(j).start())

    lax.fori_loop(depth, depth + 1, step, 0)

    def own_tile(tile, carry):
        cols = columns(tile, g)
        zt = lo + tile // 2
        yp = tile % 2
        ig_ref[:, cols] = (
            nt(dvb[0, 0], wall[zt, yp, 0])
            + nt(dvb[0, 1], wall[zt, yp, 1])
            + jnp.dot(gm[...], a_all[:, cols], preferred_element_type=F32)
        ).astype(BF16)
        return carry

    lax.fori_loop(0, 2 * half, own_tile, 0)

    def finish(tile, carry):
        wait_in(orecv.at[tile], o_r.at[tile])
        cols = columns(tile, 1 - g)
        ig_ref[:, cols] = (
            orecv[tile].astype(F32)
            + jnp.dot(gm[...], a_all[:, cols], preferred_element_type=F32)
        ).astype(BF16)
        return carry

    lax.fori_loop(0, 2 * half, finish, 0)

    lo_ref[0] = lfull[mine, :]
    ra_ref[0] = rsend[mine, :]

    def add_terms(j):
        wait_in(rrecv.at[rank_rows(j), :], r_r.at[j])
        ra_ref[0] = ra_ref[0] + rrecv[rank_rows(j), :]

    peers(add_terms)

    def add_level(zp):
        wait_in(lrecv.at[zp], l_r.at[zp])
        lo_ref[0] = lo_ref[0] + lrecv[zp].astype(F32)

    levels(add_level)

    for i in range(3):
        dv_copy(i).wait_send()
    gm_copy.wait_send()
    low_copy.wait_send()

    def sent(j):
        b_copy(j).wait_send()
        r_copy(j).wait_send()

    peers(sent)
    a_copy(f, opposite).wait_send()

    def sent_level(zp):
        a_copy(f, zp * 2 + y).wait_send()
        a_copy(opposite, zp * 2 + y).wait_send()
        l_cross(zp).wait_send()
        l_copy(zp).wait_send()

    levels(sent_level)
    l_cross(z).wait_send()

    def sent_tile(tile, carry):
        o_copy(tile).wait_send()
        return carry

    lax.fori_loop(0, 2 * half, sent_tile, 0)

    def sent_piece(zp, carry):
        @pl.when((zp <= z) & (z < depth - 1))
        def _():
            chain_copy(zp, True).wait_send()

        @pl.when((zp >= z) & (z > 0))
        def _():
            chain_copy(zp, False).wait_send()

        y_copy(zp).wait_send()

        @pl.when(zp // half != c)
        def _():
            sib_copy(zp).wait_send()

        return carry

    lax.fori_loop(0, depth, sent_piece, 0)


def fused(fsdp_total, x, dv, w, a, b, counts, storage):
    tokens, width = x.shape
    heads = dv.shape[1]
    rank = a.shape[1]
    slots = fsdp_total * rank
    depth = fsdp_total // 2
    half = depth // 2
    rows = w.shape[0] // 2
    vmem = pl.BlockSpec(memory_space=pltpu.VMEM)
    smem = pl.BlockSpec(memory_space=pltpu.SMEM)
    dma = pltpu.SemaphoreType.DMA
    n = fsdp_total
    return pl.pallas_call(
        functools.partial(fused_kernel, fsdp_total),
        out_shape=(
            jax.ShapeDtypeStruct((tokens, width), BF16),
            jax.ShapeDtypeStruct((1, rank, width), F32),
            jax.ShapeDtypeStruct((1, rank, heads), F32),
        ),
        in_specs=[vmem] * 5 + [smem] * 2,
        out_specs=(vmem,) * 3,
        scratch_shapes=[
            pltpu.VMEM((depth, 2, 2, rows, heads), BF16),
            pltpu.VMEM((2, 2, tokens, heads), BF16),
            pltpu.VMEM((slots, width), BF16),
            pltpu.VMEM((slots, heads), BF16),
            pltpu.VMEM((tokens, slots), F32),
            pltpu.VMEM((tokens, slots), BF16),
            pltpu.VMEM((slots, tokens), BF16),
            pltpu.VMEM((2, tokens, slots), F32),
            pltpu.VMEM((2, tokens, slots), F32),
            pltpu.VMEM((slots, width), BF16),
            pltpu.VMEM((depth, rank, width), BF16),
            pltpu.VMEM((depth, rank, width), BF16),
            pltpu.VMEM((slots, width), F32),
            pltpu.VMEM((slots, heads), F32),
            pltpu.VMEM((slots, heads), F32),
            pltpu.VMEM((2 * half, tokens, rows), BF16),
            pltpu.VMEM((2 * half, tokens, rows), BF16),
            dma((depth, 2)), dma((depth,)),
            dma((depth,)), dma((depth, 2)),
            dma((depth,)), dma((depth,)),
            dma((2 * n,)), dma((n,)), dma((n,)), dma((n,)),
            dma((n,)), dma((depth,)), dma((depth,)), dma((n,)), dma((n,)),
            dma((3,)), dma((3,)), dma((2,)), dma((2,)),
            dma((2 * half,)), dma((2 * half,)),
        ],
        compiler_params=pltpu.CompilerParams(
            collective_id=0, has_side_effects=True, vmem_limit_bytes=60 * 1024 * 1024
        ),
    )(x, dv, w, a, b, counts, storage)


def solution(mesh):
    in_specs = (
        P(("group", "fsdp"), "tp"),
        P(("group", "fsdp"), "tp"),
        P("fsdp", "tp"),
        P(("group", "fsdp"), None, "tp"),
        P(("group", "fsdp"), None, "tp"),
        P("group"),
        P("group"),
    )
    out_specs = (
        P(("group", "fsdp"), "tp"),
        P(("group", "fsdp"), None, "tp"),
        P(("group", "fsdp"), None, "tp"),
    )
    shape = dict(mesh.shape)
    paired = shape["group"] == 2 and shape["fsdp"] == 8 and shape["tp"] == 2
    body = functools.partial(fused, shape["fsdp"]) if paired else shards
    return jax.shard_map(body, mesh=mesh, in_specs=in_specs, out_specs=out_specs, check_vma=False)
```

```python
import functools

import jax
import jax.numpy as jnp
from jax import lax
from jax.experimental import pallas as pl
from jax.experimental.pallas import tpu as pltpu
from jax.sharding import PartitionSpec as P

BLOCK = 128


adapter_scale = 2.0


def shards(
    inputs,
    value_gradient,
    fixed_projection_matrix,
    adapter_down_weight,
    adapter_up_weight,
    live_token_count,
    adapter_storage_row,
):
    token_rows = inputs.shape[0]
    half_width = inputs.shape[1]
    heads_half = value_gradient.shape[1]
    adapter_total = live_token_count.shape[0]
    block_count = token_rows // BLOCK
    place_offset = lax.axis_index("fsdp")
    blocks_of = (live_token_count + BLOCK - 1) // BLOCK
    stop_marks = jnp.cumsum(blocks_of)
    firsts = stop_marks - blocks_of
    segment_labels = place_offset * block_count + jnp.arange(block_count, dtype=jnp.int32)
    owner_adapter = jnp.sum(
        (stop_marks[None, :] <= segment_labels[:, None]).astype(jnp.int32), axis=1
    )
    owner_hot = jnp.arange(adapter_total, dtype=jnp.int32)[None, :] == owner_adapter[:, None]
    count_block = jnp.sum(jnp.where(owner_hot, live_token_count[None, :], 0), axis=1)
    first_block = jnp.sum(jnp.where(owner_hot, firsts[None, :], 0), axis=1)
    position_segment = jnp.sum(jnp.where(owner_hot, adapter_storage_row[None, :], 0), axis=1)
    offsets = jnp.arange(BLOCK, dtype=jnp.int32)
    live = (segment_labels[:, None] - first_block[:, None]) * BLOCK + offsets[
        None, :
    ] < count_block[:, None]
    grad_blocks = value_gradient.reshape(block_count, BLOCK, heads_half)
    masked_tokens = jnp.where(live[:, :, None], grad_blocks, jnp.zeros_like(grad_blocks))
    source_segments = inputs.reshape(block_count, BLOCK, half_width)
    every_lowering_factor, up_all = (
        lax.all_gather(adapter_down_weight, "fsdp", axis=0, tiled=True),
        lax.all_gather(adapter_up_weight, "fsdp", axis=0, tiled=True),
    )
    picked_lowering_factor = jnp.take(every_lowering_factor, position_segment, axis=0)
    up_sel = jnp.take(up_all, position_segment, axis=0)
    low_part = jnp.einsum(
        "nsm,nxm->nsx", source_segments, picked_lowering_factor, preferred_element_type=jnp.float32
    )
    inner_grad_piece = jnp.einsum(
        "btk,brk->btr", masked_tokens, up_sel, preferred_element_type=jnp.float32
    )
    low_sum, middle_gradient_sum = lax.psum((low_part, inner_grad_piece), "tp")
    reduced_activation = low_sum.astype(jnp.bfloat16)
    narrow_backflow = (adapter_scale * middle_gradient_sum).astype(jnp.bfloat16)
    adapter_contribution = jnp.einsum(
        "njc,ncd->njd", narrow_backflow, picked_lowering_factor, preferred_element_type=jnp.float32
    )
    down_terms = jnp.einsum(
        "btr,bth->brh", narrow_backflow, source_segments, preferred_element_type=jnp.float32
    )
    up_contributions = adapter_scale * jnp.einsum(
        "btr,btk->brk", reduced_activation, masked_tokens, preferred_element_type=jnp.float32
    )
    slot_hot = (
        jnp.arange(adapter_total, dtype=jnp.int32)[None, :] == position_segment[:, None]
    ).astype(jnp.float32)
    dense_down = jnp.einsum("ba,brh->arh", slot_hot, down_terms, precision=lax.Precision.HIGHEST)
    dense_up = jnp.einsum(
        "ba,brk->ark", slot_hot, up_contributions, precision=lax.Precision.HIGHEST
    )
    sent_down = dense_down[:, None, :, :]
    sent_up = dense_up[:, None, :, :]
    recv_down, recv_up = (
        lax.all_to_all(sent_down, "fsdp", split_axis=0, concat_axis=1, tiled=True),
        lax.all_to_all(sent_up, "fsdp", split_axis=0, concat_axis=1, tiled=True),
    )
    lowering_sensitivity = jnp.sum(recv_down, axis=1)
    raising_sensitivity = jnp.sum(recv_up, axis=1)
    masked_rows = masked_tokens.reshape(token_rows, heads_half)
    every_feature = lax.dot_general(
        masked_rows,
        lax.all_gather(fixed_projection_matrix, "fsdp", axis=0, tiled=True),
        (((1,), (1,)), ((), ())),
        preferred_element_type=jnp.float32,
    )
    frozen_output = lax.psum_scatter(every_feature, "tp", scatter_dimension=1, tiled=True)
    input_gradient = (frozen_output + adapter_contribution.reshape(token_rows, half_width)).astype(
        jnp.bfloat16
    )
    return (input_gradient, lowering_sensitivity, raising_sensitivity)


F32 = jnp.float32
BF16 = jnp.bfloat16
CUTS = 2


def nt(a, b):
    return lax.dot_general(a, b, (((1,), (1,)), ((), ())), preferred_element_type=F32)


def fused_kernel(
    fsdp_total,
    x_ref, dv_ref, w_ref, a_ref, b_ref, cnt_ref, row_ref,
    ig_ref, lo_ref, ra_ref,
    wall, dvb, a_all, b_all, mask, gm, gm_t, psend, precv,
    lsend, lcross, lrecv, lfull, rsend, rrecv, osend, orecv,
    ch_s, ch_r, y_s, y_r, sb_s, sb_r, a_s, a_r, b_s, b_r,
    l_s, lc_r, l_r, r_s, r_r, dv_s, dv_r, p_s, p_r, o_s, o_r,
):
    depth = fsdp_total // 2
    half = depth // 2
    tokens, width = x_ref.shape
    heads = dv_ref.shape[1]
    rank = a_ref.shape[1]
    slots = fsdp_total * rank
    rows = w_ref.shape[0] // 2
    part_rows = rows // CUTS
    g = lax.axis_index("group")
    f = lax.axis_index("fsdp")
    c = lax.axis_index("tp")
    z = f // 2
    y = f % 2
    lo = c * half
    sibling = (g, f, 1 - c)
    twin = (1 - g, f, c)

    def remote(src, dst, ss, rs, dev):
        return pltpu.make_async_remote_copy(
            src_ref=src, dst_ref=dst, send_sem=ss, recv_sem=rs,
            device_id=dev, device_id_type=pl.DeviceIdType.MESH,
        )

    barrier = pltpu.get_barrier_semaphore()
    for k in range(1, fsdp_total):
        pl.semaphore_signal(
            barrier, inc=1, device_id=(g, lax.rem(f + k, fsdp_total), c),
            device_id_type=pl.DeviceIdType.MESH,
        )
    for dev in (sibling, twin, (g, z * 2 + 1 - y, 1 - c)):
        pl.semaphore_signal(barrier, inc=1, device_id=dev, device_id_type=pl.DeviceIdType.MESH)

    for h in range(CUTS):
        at = pl.multiple_of(g * rows + h * part_rows, part_rows)
        wall[z * CUTS + h, y, c] = w_ref[pl.ds(at, part_rows), :]
    mine = pl.ds(pl.multiple_of(f * rank, rank), rank)
    a_all[mine, :] = a_ref[0]
    b_all[mine, :] = b_ref[0]
    token = f * tokens + lax.broadcasted_iota(jnp.int32, (tokens, slots), 0)
    lane_row = lax.broadcasted_iota(jnp.int32, (tokens, slots), 1) // rank
    start = jnp.int32(0)
    alive = jnp.zeros((tokens, slots), F32)
    any_live = jnp.zeros((tokens, slots), F32)
    for a in range(fsdp_total):
        count = cnt_ref[a]
        blocks = (count + (BLOCK - 1)) // BLOCK
        inside = jnp.where((token >= start) & (token < start + count), 1.0, 0.0)
        any_live = any_live + inside
        alive = alive + jnp.where(lane_row == row_ref[a], inside, 0.0)
        start = start + blocks * BLOCK
    mask[...] = alive
    live_column = any_live[:, :1]
    dvb[0, c] = jnp.where(live_column > 0.5, dv_ref[...].astype(F32), 0.0).astype(BF16)

    pl.semaphore_wait(barrier, fsdp_total + 2)

    def dv_copy(i):
        if i == 0:
            return remote(dvb.at[0, c], dvb.at[0, c], dv_s.at[0], dv_r.at[0], sibling)
        if i == 1:
            return remote(dvb.at[0, c], dvb.at[1, c], dv_s.at[1], dv_r.at[1], twin)
        return remote(dvb.at[1, c], dvb.at[1, c], dv_s.at[2], dv_r.at[2], sibling)

    def piece(q):
        return wall.at[q, y, c]

    def chain_copy(q, up):
        to = z + 1 if up else z - 1
        return remote(piece(q), piece(q), ch_s.at[q, 1 if up else 0], ch_r.at[q], (g, to * 2 + y, c))

    def y_copy(q):
        core = q // (half * CUTS)
        return remote(piece(q), piece(q), y_s.at[q], y_r.at[q, c], (g, z * 2 + 1 - y, core))

    def sib_copy(q):
        return remote(piece(q), piece(q), sb_s.at[q], sb_r.at[q], sibling)

    def b_copy(j):
        return remote(b_all.at[mine, :], b_all.at[mine, :], b_s.at[j], b_r.at[f], (g, j, c))

    opposite = z * 2 + 1 - y

    def a_copy(s, j):
        part = a_all.at[rank_rows(s), :]
        return remote(part, part, a_s.at[j * 2 + s % 2], a_r.at[s], (g, j, c))

    def levels(fn):
        def step(k, carry):
            fn(lax.rem(z + k, depth))
            return carry
        lax.fori_loop(1, depth, step, 0)

    def peers(fn):
        def step(k, carry):
            fn(lax.rem(f + k, fsdp_total))
            return carry
        lax.fori_loop(1, fsdp_total, step, 0)

    def rank_rows(j):
        return pl.ds(pl.multiple_of(j * rank, rank), rank)

    def wait_in(dst, sem):
        remote(dst, dst, sem, sem, sibling).wait_recv()

    def spread(q):
        y_copy(q).start()

        @pl.when(q // (half * CUTS) != c)
        def _():
            sib_copy(q).start()

    dv_copy(0).start()
    peers(lambda j: b_copy(j).start())

    @pl.when(z < depth - 1)
    def _():
        for h in range(CUTS):
            chain_copy(z * CUTS + h, True).start()

    @pl.when(z > 0)
    def _():
        for h in range(CUTS):
            chain_copy(z * CUTS + h, False).start()

    dv_copy(1).start()
    for h in range(CUTS):
        spread(z * CUTS + h)

    peers(lambda j: wait_in(b_all.at[rank_rows(j), :], b_r.at[j]))
    psend[0] = nt(dvb[0, c], b_all[...])
    gm_copy = remote(psend.at[0], precv.at[0], p_s.at[0], p_r.at[0], sibling)
    gm_copy.start()
    gm_copy.wait_recv()
    total = adapter_scale * (psend[0] + precv[0])
    total = jnp.where(mask[...] > 0.5, total, 0.0)
    gm[...] = total.astype(BF16)
    gm_t[...] = total.T.astype(BF16)

    chunk = 512

    def lower(i, carry):
        cols = pl.ds(pl.multiple_of(i * chunk, chunk), chunk)
        term = jnp.dot(gm_t[...], x_ref[:, cols], preferred_element_type=F32)
        lfull[:, cols] = term
        lsend[:, cols] = term.astype(BF16)
        return carry

    lax.fori_loop(0, width // chunk, lower, 0)

    def l_cross(zp):
        return remote(
            lsend.at[rank_rows(zp * 2 + 1 - y), :], lcross.at[zp], l_s.at[zp * 2 + 1 - y], lc_r.at[zp], (g, opposite, c)
        )

    def l_copy(zp):
        return remote(
            lsend.at[rank_rows(zp * 2 + y), :], lrecv.at[z], l_s.at[zp * 2 + y], l_r.at[z], (g, zp * 2 + y, c)
        )

    levels(lambda zp: l_cross(zp).start())
    l_cross(z).start()


    wait_in(dvb.at[1, c], dv_r.at[1])
    dv_copy(2).start()

    wait_in(dvb.at[0, 1 - c], dv_r.at[0])
    wait_in(dvb.at[1, 1 - c], dv_r.at[2])

    def join(zp):
        wait_in(lcross.at[zp], lc_r.at[zp])
        place = rank_rows(zp * 2 + y)
        lfull[place, :] = lfull[place, :] + lcross[zp].astype(F32)
        lsend[place, :] = lfull[place, :].astype(BF16)
        l_copy(zp).start()

    def join_all():
        levels(join)
        wait_in(lcross.at[z], lc_r.at[z])
        lfull[mine, :] = lfull[mine, :] + lcross[z].astype(F32)

    def o_copy(tile):
        return remote(osend.at[tile], orecv.at[tile], o_s.at[tile], o_r.at[tile], twin)

    def columns(tile, which):
        at = (tile // CUTS) * (2 * rows) + which * rows + (tile % CUTS) * part_rows
        return pl.ds(pl.multiple_of(at, part_rows), part_rows)

    def tiles(zt):
        for h in range(CUTS):
            q = zt * CUTS + h
            wait_in(wall.at[q, y, 1 - c], sb_r.at[q])
            for other in (0, 1):
                yp = 1 - y if other else y
                if other:
                    wait_in(wall.at[q, yp, 0], y_r.at[q, 0])
                    wait_in(wall.at[q, yp, 1], y_r.at[q, 1])
                tile = ((zt - lo) * 2 + yp) * CUTS + h
                osend[tile] = (nt(dvb[1, 0], wall[q, yp, 0]) + nt(dvb[1, 1], wall[q, yp, 1])).astype(BF16)
                o_copy(tile).start()

    def in_half(zp):
        return (zp >= lo) & (zp < lo + half)

    def step(d, carry):
        for h in range(CUTS):

            @pl.when(z - d >= 0)
            def _(h=h):
                q = (z - d) * CUTS + h
                wait_in(piece(q), ch_r.at[q])

                @pl.when(z < depth - 1)
                def _():
                    chain_copy(q, True).start()

                spread(q)

            @pl.when(z + d < depth)
            def _(h=h):
                q = (z + d) * CUTS + h
                wait_in(piece(q), ch_r.at[q])

                @pl.when(z > 0)
                def _():
                    chain_copy(q, False).start()

                spread(q)

        zt = jnp.where(in_half(z + d - 1), z + d - 1, z - d + 1)

        @pl.when(in_half(zt))
        def _():
            tiles(zt)

        return carry

    lax.fori_loop(1, 2, step, 0)
    join_all()
    a_copy(f, opposite).start()
    lax.fori_loop(2, 3, step, 0)
    levels(lambda zp: a_copy(f, zp * 2 + y).start())
    lax.fori_loop(3, depth, step, 0)

    wait_in(a_all.at[rank_rows(opposite), :], a_r.at[opposite])
    levels(lambda zp: a_copy(opposite, zp * 2 + y).start())
    lax.fori_loop(depth, depth + 1, step, 0)

    levels(lambda zp: wait_in(a_all.at[rank_rows(zp * 2 + y), :], a_r.at[zp * 2 + y]))
    levels(lambda zp: wait_in(a_all.at[rank_rows(zp * 2 + 1 - y), :], a_r.at[zp * 2 + 1 - y]))
    psend[1] = jnp.zeros((tokens, slots), F32)

    def low_step(i, carry):
        cols = pl.ds(pl.multiple_of(i * chunk, chunk), chunk)
        psend[1] = psend[1] + nt(x_ref[:, cols], a_all[:, cols])
        return carry

    lax.fori_loop(0, width // chunk, low_step, 0)
    low_copy = remote(psend.at[1], precv.at[1], p_s.at[1], p_r.at[1], sibling)
    low_copy.start()
    def own_tile(tile, carry):
        cols = columns(tile, g)
        q = (lo + tile // (2 * CUTS)) * CUTS + tile % CUTS
        yp = (tile // CUTS) % 2
        ig_ref[:, cols] = (
            nt(dvb[0, 0], wall[q, yp, 0])
            + nt(dvb[0, 1], wall[q, yp, 1])
            + jnp.dot(gm[...], a_all[:, cols], preferred_element_type=F32)
        ).astype(BF16)
        return carry

    lax.fori_loop(0, 2 * half * CUTS, own_tile, 0)

    low_copy.wait_recv()
    low = jnp.where(mask[...] > 0.5, psend[1] + precv[1], 0.0)
    up_term = adapter_scale * jnp.dot(low.T.astype(BF16), dvb[0, c], preferred_element_type=F32)
    rsend[...] = up_term

    def r_copy(j):
        return remote(rsend.at[rank_rows(j), :], rrecv.at[mine, :], r_s.at[j], r_r.at[f], (g, j, c))

    peers(lambda j: r_copy(j).start())

    def finish(tile, carry):
        wait_in(orecv.at[tile], o_r.at[tile])
        cols = columns(tile, 1 - g)
        ig_ref[:, cols] = (
            orecv[tile].astype(F32)
            + jnp.dot(gm[...], a_all[:, cols], preferred_element_type=F32)
        ).astype(BF16)
        return carry

    lax.fori_loop(0, 2 * half * CUTS, finish, 0)

    lo_ref[0] = lfull[mine, :]
    ra_ref[0] = rsend[mine, :]

    def add_terms(j):
        wait_in(rrecv.at[rank_rows(j), :], r_r.at[j])
        ra_ref[0] = ra_ref[0] + rrecv[rank_rows(j), :]

    peers(add_terms)

    def add_level(zp):
        wait_in(lrecv.at[zp], l_r.at[zp])
        lo_ref[0] = lo_ref[0] + lrecv[zp].astype(F32)

    levels(add_level)

    for i in range(3):
        dv_copy(i).wait_send()
    gm_copy.wait_send()
    low_copy.wait_send()

    def sent(j):
        b_copy(j).wait_send()
        r_copy(j).wait_send()

    peers(sent)
    a_copy(f, opposite).wait_send()

    def sent_level(zp):
        a_copy(f, zp * 2 + y).wait_send()
        a_copy(opposite, zp * 2 + y).wait_send()
        l_cross(zp).wait_send()
        l_copy(zp).wait_send()

    levels(sent_level)
    l_cross(z).wait_send()

    def sent_tile(tile, carry):
        o_copy(tile).wait_send()
        return carry

    lax.fori_loop(0, 2 * half * CUTS, sent_tile, 0)

    def sent_piece(q, carry):
        @pl.when((q // CUTS <= z) & (z < depth - 1))
        def _():
            chain_copy(q, True).wait_send()

        @pl.when((q // CUTS >= z) & (z > 0))
        def _():
            chain_copy(q, False).wait_send()

        y_copy(q).wait_send()

        @pl.when(q // (half * CUTS) != c)
        def _():
            sib_copy(q).wait_send()

        return carry

    lax.fori_loop(0, depth * CUTS, sent_piece, 0)


def fused(fsdp_total, x, dv, w, a, b, counts, storage):
    tokens, width = x.shape
    heads = dv.shape[1]
    rank = a.shape[1]
    slots = fsdp_total * rank
    depth = fsdp_total // 2
    half = depth // 2
    rows = w.shape[0] // 2
    vmem = pl.BlockSpec(memory_space=pltpu.VMEM)
    smem = pl.BlockSpec(memory_space=pltpu.SMEM)
    dma = pltpu.SemaphoreType.DMA
    n = fsdp_total
    return pl.pallas_call(
        functools.partial(fused_kernel, fsdp_total),
        out_shape=(
            jax.ShapeDtypeStruct((tokens, width), BF16),
            jax.ShapeDtypeStruct((1, rank, width), F32),
            jax.ShapeDtypeStruct((1, rank, heads), F32),
        ),
        in_specs=[vmem] * 5 + [smem] * 2,
        out_specs=(vmem,) * 3,
        scratch_shapes=[
            pltpu.VMEM((depth * CUTS, 2, 2, rows // CUTS, heads), BF16),
            pltpu.VMEM((2, 2, tokens, heads), BF16),
            pltpu.VMEM((slots, width), BF16),
            pltpu.VMEM((slots, heads), BF16),
            pltpu.VMEM((tokens, slots), F32),
            pltpu.VMEM((tokens, slots), BF16),
            pltpu.VMEM((slots, tokens), BF16),
            pltpu.VMEM((2, tokens, slots), F32),
            pltpu.VMEM((2, tokens, slots), F32),
            pltpu.VMEM((slots, width), BF16),
            pltpu.VMEM((depth, rank, width), BF16),
            pltpu.VMEM((depth, rank, width), BF16),
            pltpu.VMEM((slots, width), F32),
            pltpu.VMEM((slots, heads), F32),
            pltpu.VMEM((slots, heads), F32),
            pltpu.VMEM((2 * half * CUTS, tokens, rows // CUTS), BF16),
            pltpu.VMEM((2 * half * CUTS, tokens, rows // CUTS), BF16),
            dma((depth * CUTS, 2)), dma((depth * CUTS,)),
            dma((depth * CUTS,)), dma((depth * CUTS, 2)),
            dma((depth * CUTS,)), dma((depth * CUTS,)),
            dma((2 * n,)), dma((n,)), dma((n,)), dma((n,)),
            dma((n,)), dma((depth,)), dma((depth,)), dma((n,)), dma((n,)),
            dma((3,)), dma((3,)), dma((2,)), dma((2,)),
            dma((2 * half * CUTS,)), dma((2 * half * CUTS,)),
        ],
        compiler_params=pltpu.CompilerParams(
            collective_id=0, has_side_effects=True, vmem_limit_bytes=60 * 1024 * 1024
        ),
    )(x, dv, w, a, b, counts, storage)


def solution(mesh):
    in_specs = (
        P(("group", "fsdp"), "tp"),
        P(("group", "fsdp"), "tp"),
        P("fsdp", "tp"),
        P(("group", "fsdp"), None, "tp"),
        P(("group", "fsdp"), None, "tp"),
        P("group"),
        P("group"),
    )
    out_specs = (
        P(("group", "fsdp"), "tp"),
        P(("group", "fsdp"), None, "tp"),
        P(("group", "fsdp"), None, "tp"),
    )
    shape = dict(mesh.shape)
    paired = shape["group"] == 2 and shape["fsdp"] == 8 and shape["tp"] == 2
    body = functools.partial(fused, shape["fsdp"]) if paired else shards
    return jax.shard_map(body, mesh=mesh, in_specs=in_specs, out_specs=out_specs, check_vma=False)
```
